32 devices in a mesh: ctx: 4 (over y, core), ch: 8 (over z, x).
Axes of the slice: x: 2, y: 2, z: 4, core: 2. Of those that a mesh axis runs over, the one named last changes fastest.
Arguments:
- query: bfloat16 [128, 4096], P('ch', 'ctx'), may hold values from -16 to 16
- key_branch: bfloat16 [128, 4096], P('ch', 'ctx'), may hold values from -6 to 6
- value_branch: bfloat16 [128, 4096], P('ch', 'ctx'), may hold values from -6 to 6
- residue: float32 [128, 16], P('ch'), may hold values from -1.5 to 1.5
- rate: float32 [128, 16], P('ch'), may hold values from 6.1035156e-05 to 0.03
- skip: float32 [128], P('ch'), may hold values from -4 to 4
- gain: float32 [128], P('ch'), may hold values from 0.1 to 1.9
Outputs:
- mixed_out: bfloat16 [128, 4096], P('ch', 'ctx')
The draws below stay inside these ranges and needn't reach their ends.
All inputs are finite; a program needn't handle non-finite values.
Results may differ from the reference program's by a relative error of at most 0.009.
Values may be sent and summed in bfloat16 or wider, within the bound.
A program may use at most 64 MiB of HBM per device.

```python
import jax
import jax.numpy as jnp
from jax import lax

MODES = 16
CH = 128
SEQ = 4096


def draw_rate(key, part):
    picker = jax.random.uniform(jax.random.fold_in(key, 11), (CH, MODES))
    unit_draw = jax.random.uniform(jax.random.fold_in(key, 12), (CH, MODES))
    slow_share = 0.5
    slow_rate = jnp.exp(jnp.log(0.25 / SEQ) + unit_draw * jnp.log(8.0))
    fast_rate = jnp.exp(jnp.log(2.0 / SEQ) + unit_draw * (jnp.log(0.03) - jnp.log(2.0 / SEQ)))
    return jnp.where(picker < slow_share, slow_rate, fast_rate).astype(jnp.float32)


def draw_query(key, part):
    channel_pos = jnp.arange(CH, dtype=jnp.float32) / (CH - 1)
    base_vals = jax.random.truncated_normal(jax.random.fold_in(key, 22), -4.0, 4.0, (CH, SEQ))
    scales = 3.0 ** channel_pos
    return (base_vals * scales[:, None]).astype(jnp.bfloat16)


def block_levels(rng, dims, cuts, least, top_value):
    factor_of, own = 1.0, jax.random.fold_in(rng, 6)
    for dim, shards_of in cuts:
        steps = jnp.exp(jax.random.uniform(jax.random.fold_in(own, dim), (shards_of,), jnp.float32, least / len(cuts), top_value / len(cuts)))
        factor_of = factor_of * jnp.repeat(steps, dims[dim] // shards_of).reshape([-1 if axis == dim else 1 for axis in range(len(dims))])
    return factor_of


def scatter_about(rng, extent, width, bound, split=(), kind=jnp.bfloat16):
    values = width * jax.random.normal(rng, extent, jnp.float32)
    if split:
        values = values * block_levels(rng, extent, split, -0.22, 0.18)
    return jnp.clip(values, -bound, bound).astype(kind)


def setup_inputs(seed: int = 0) -> dict:
    seeds = jax.random.split(jax.random.key(seed), 8)
    query = draw_query(jax.random.fold_in(seeds[7], 71), 0)
    key_branch = scatter_about(seeds[1], (CH, SEQ), 1.0, 6.0, ((0, 8), (1, 4)))
    value_branch = scatter_about(seeds[2], (CH, SEQ), 1.0, 6.0, ((0, 8), (1, 4)))
    residue = scatter_about(seeds[3], (CH, MODES), MODES ** -0.5, 1.5, ((0, 8),), jnp.float32)
    rate = draw_rate(jax.random.fold_in(seeds[7], 71), 0)
    skip = scatter_about(seeds[5], (CH,), 1.0, 4.0, ((0, 8),), jnp.float32)
    gain = jnp.clip(1.0 + 0.18 * jax.random.normal(seeds[6], (CH,), jnp.float32), 0.1, 1.9)
    return {"query": query, "key_branch": key_branch, "value_branch": value_branch, "residue": residue, "rate": rate, "skip": skip, "gain": gain}


def modal_taps(lags, residue, rate):
    lag_float = jnp.maximum(lags, 0).astype(jnp.float32)
    scaled = jnp.sqrt(-jnp.expm1(-2.0 * rate)) * residue

    def add_mode(index, total):
        return total + scaled[:, index][:, None] * jnp.exp(-rate[:, index][:, None] * lag_float[None, :])
    start_total = jnp.zeros((residue.shape[0], lags.shape[0]), jnp.float32)
    total = lax.fori_loop(0, residue.shape[1], add_mode, start_total)
    return jnp.where((lags >= 0)[None, :], total, 0.0)

def reference(query, key_branch, value_branch, residue, rate, skip, gain):
    signal = (key_branch * value_branch).astype(jnp.bfloat16)
    lags = jnp.arange(SEQ, dtype=jnp.int32)
    taps = modal_taps(lags, residue, rate)
    signal_float = signal.astype(jnp.float32)
    spec_taps = jnp.fft.rfft(taps, n=2 * SEQ, axis=1)
    spec_signal = jnp.fft.rfft(signal_float, n=2 * SEQ, axis=1)
    conv = jnp.fft.irfft(spec_taps * spec_signal, n=2 * SEQ, axis=1)[:, :SEQ]
    mixed = query.astype(jnp.float32) * (conv + skip[:, None] * signal_float)
    mean_square = lax.optimization_barrier(jnp.mean(mixed * mixed, axis=0, keepdims=True))
    return (mixed / jnp.sqrt(mean_square + 1e-06) * gain[:, None]).astype(jnp.bfloat16)
```

```python
import functools

import jax
import jax.numpy as jnp
from jax import lax
from jax.experimental import pallas as pl
from jax.experimental.pallas import tpu as pltpu
from jax.sharding import PartitionSpec as P

F32 = jnp.float32
BF16 = jnp.bfloat16
MESH = pl.DeviceIdType.MESH
CHUNK = 128


def split(value):
    high = value.astype(BF16)
    return high, (value - high.astype(F32)).astype(BF16)


def dot(left, right):
    return jnp.dot(left, right, preferred_element_type=F32)


def dot_nt(left, right):
    return lax.dot_general(left, right, (((1,), (1,)), ((), ())), preferred_element_type=F32)


def one_minus_exp(x):
    series = jnp.ones_like(x)
    for order in range(10, 1, -1):
        series = 1.0 - x * (1.0 / order) * series
    return jnp.where(x < 0.25, x * series, 1.0 - jnp.exp(-x))


def column(row, rows):
    width = row.shape[1]
    keep = lax.broadcasted_iota(jnp.int32, (rows, width), 0) == lax.broadcasted_iota(
        jnp.int32, (rows, width), 1
    )
    return jnp.sum(jnp.where(keep, row, 0.0), axis=1, keepdims=True)


def kernel(
    n_ctx, n_ch, query_hbm, key_hbm, value_hbm, residue_hbm, rate_hbm, skip_hbm, gain_hbm, out_ref,
    query_ref, key_ref, value_ref, residue_ref, rate_ref, skip_ref, gain_ref,
    toeplitz, spread, state, state_slots, square, square_slots,
    in_sems, state_send, state_recv, square_send, square_recv,
):
    my_ctx, my_ch = lax.axis_index("ctx"), lax.axis_index("ch")
    channels, block = query_ref.shape
    modes = rate_ref.shape[1]
    width = channels * modes
    chunks = block // CHUNK

    loads = [
        pltpu.make_async_copy(src, dst, in_sems.at[i])
        for i, (src, dst) in enumerate(
            (
                (rate_hbm, rate_ref), (residue_hbm, residue_ref), (key_hbm, key_ref),
                (value_hbm, value_ref), (skip_hbm, skip_ref), (gain_hbm, gain_ref),
                (query_hbm, query_ref),
            )
        )
    ]
    for load in loads:
        load.start()

    barrier = pltpu.get_barrier_semaphore()
    for step in range(1, n_ctx):
        pl.semaphore_signal(
            barrier, inc=1, device_id={"ctx": lax.rem(my_ctx + step, n_ctx)}, device_id_type=MESH
        )
    for step in range(1, n_ch):
        pl.semaphore_signal(
            barrier, inc=1, device_id={"ch": lax.rem(my_ch + step, n_ch)}, device_id_type=MESH
        )

    loads[0].wait()
    loads[1].wait()
    lane = lax.broadcasted_iota(jnp.int32, (channels, width), 1)
    own = lane // modes == lax.broadcasted_iota(jnp.int32, (channels, width), 0)
    mode_lane = lax.broadcasted_iota(jnp.int32, (modes, width), 1)
    mode_row = lax.broadcasted_iota(jnp.int32, (modes, width), 0)
    pick = (lax.rem(mode_lane, modes) == mode_row).astype(F32)
    tiled = jnp.dot(
        jnp.concatenate([rate_ref[...], residue_ref[...]], axis=0), pick,
        precision=lax.Precision.HIGHEST, preferred_element_type=F32,
    )
    rate_tiled, residue_tiled = tiled[:channels], tiled[channels:]
    rate_row = jnp.sum(jnp.where(own, rate_tiled, 0.0), axis=0, keepdims=True)
    place = lax.broadcasted_iota(jnp.int32, (CHUNK, width), 0).astype(F32)
    tail_high, tail_low = split(jnp.exp(-rate_row * (CHUNK - place)))
    chunk_decay = jnp.exp(-rate_row * float(CHUNK))

    loads[2].wait()
    loads[3].wait()
    pieces = [
        key_ref[:, k * CHUNK:(k + 1) * CHUNK] * value_ref[:, k * CHUNK:(k + 1) * CHUNK]
        for k in range(chunks)
    ]
    signal = jnp.concatenate(pieces, axis=0)
    update = dot(signal, tail_high) + dot(signal, tail_low)
    held = jnp.zeros((channels, width), F32)
    states = []
    for k in range(chunks):
        states.append(held)
        held = chunk_decay * held + update[k * channels:(k + 1) * channels]
    state[...] = jnp.sum(jnp.where(own, held, 0.0), axis=0, keepdims=True)

    pl.semaphore_wait(barrier, n_ctx + n_ch - 2)
    state_copies = [
        pltpu.make_async_remote_copy(
            src_ref=state, dst_ref=state_slots.at[step - 1],
            send_sem=state_send.at[step - 1], recv_sem=state_recv.at[step - 1],
            device_id={"ctx": lax.rem(my_ctx + step, n_ctx)}, device_id_type=MESH,
        )
        for step in range(1, n_ctx)
    ]
    for copy in state_copies:
        copy.start()

    head_high, head_low = split(jnp.exp(-rate_row * place))
    scaled = jnp.where(own, jnp.sqrt(one_minus_exp(2.0 * rate_tiled)) * residue_tiled, 0.0)
    scaled_high, scaled_low = split(scaled)
    taps = (
        dot_nt(scaled_high, head_high) + dot_nt(scaled_high, head_low)
        + dot_nt(scaled_low, head_high)
    )
    loads[4].wait()
    loads[5].wait()
    first = lax.broadcasted_iota(jnp.int32, (channels, CHUNK), 1) == 0
    taps = taps + jnp.where(first, column(skip_ref[...], channels), 0.0)
    gain = column(gain_ref[...], channels)
    causal = lax.broadcasted_iota(jnp.int32, (CHUNK, CHUNK), 1) >= lax.broadcasted_iota(
        jnp.int32, (CHUNK, CHUNK), 0
    )
    rows = lax.broadcasted_iota(jnp.int32, (channels, CHUNK), 0)
    for c in range(channels):
        rolled = pltpu.roll(
            jnp.broadcast_to(taps[c:c + 1], (CHUNK, CHUNK)), 0, 1, stride=1, stride_axis=0
        )
        toeplitz[c * CHUNK:(c + 1) * CHUNK, :] = jnp.where(causal, rolled, 0.0).astype(BF16)
        this = (rows == c).astype(F32).astype(BF16)
        for k in range(chunks):
            spread[k * channels:(k + 1) * channels, c * CHUNK:(c + 1) * CHUNK] = pieces[k] * this
    near = dot(spread[...], toeplitz[...])
    loads[6].wait()

    carry = jnp.zeros((1, width), F32)
    for step in range(1, n_ctx):
        state_copies[step - 1].wait_recv()
        weight = (my_ctx >= step).astype(F32)
        carry = carry + weight * jnp.exp(-rate_row * float(block * (step - 1))) * state_slots[step - 1]
    full = jnp.concatenate(
        [
            (states[k] + jnp.exp(-rate_row * float(CHUNK * k)) * carry) * scaled
            for k in range(chunks)
        ],
        axis=0,
    )
    full_high, full_low = split(full)
    conv = near + (
        dot_nt(full_high, head_high) + dot_nt(full_high, head_low) + dot_nt(full_low, head_high)
    )
    mixed = []
    for k in range(chunks):
        part = query_ref[:, k * CHUNK:(k + 1) * CHUNK].astype(F32) * conv[k * channels:(k + 1) * channels]
        mixed.append(part)
        square[k:k + 1, :] = jnp.sum(part * part, axis=0, keepdims=True)

    square_copies = [
        pltpu.make_async_remote_copy(
            src_ref=square, dst_ref=square_slots.at[step - 1],
            send_sem=square_send.at[step - 1], recv_sem=square_recv.at[step - 1],
            device_id={"ch": lax.rem(my_ch + step, n_ch)}, device_id_type=MESH,
        )
        for step in range(1, n_ch)
    ]
    for copy in square_copies:
        copy.start()
    total = square[...]
    for step in range(1, n_ch):
        square_copies[step - 1].wait_recv()
        total = total + square_slots[step - 1]
    scale = lax.rsqrt(total * (1.0 / (channels * n_ch)) + 1e-06)
    for k in range(chunks):
        out_ref[:, k * CHUNK:(k + 1) * CHUNK] = (mixed[k] * scale[k:k + 1] * gain).astype(BF16)
    for copy in state_copies + square_copies:
        copy.wait_send()


def body(mesh_shape, query, key_branch, value_branch, residue, rate, skip, gain):
    n_ctx, n_ch = mesh_shape
    channels, block = query.shape
    modes = rate.shape[1]
    width = channels * modes
    chunks = block // CHUNK
    arrays = (
        query, key_branch, value_branch, residue, rate,
        skip.reshape(1, channels), gain.reshape(1, channels),
    )
    return pl.pallas_call(
        functools.partial(kernel, n_ctx, n_ch),
        out_shape=jax.ShapeDtypeStruct((channels, block), BF16),
        in_specs=[pl.BlockSpec(memory_space=pl.ANY)] * len(arrays),
        out_specs=pl.BlockSpec(memory_space=pltpu.VMEM),
        scratch_shapes=[pltpu.VMEM(a.shape, a.dtype) for a in arrays] + [
            pltpu.VMEM((channels * CHUNK, CHUNK), BF16),
            pltpu.VMEM((chunks * channels, channels * CHUNK), BF16),
            pltpu.VMEM((1, width), F32),
            pltpu.VMEM((n_ctx - 1, 1, width), F32),
            pltpu.VMEM((chunks, CHUNK), F32),
            pltpu.VMEM((n_ch - 1, chunks, CHUNK), F32),
            pltpu.SemaphoreType.DMA((len(arrays),)),
            pltpu.SemaphoreType.DMA((n_ctx - 1,)),
            pltpu.SemaphoreType.DMA((n_ctx - 1,)),
            pltpu.SemaphoreType.DMA((n_ch - 1,)),
            pltpu.SemaphoreType.DMA((n_ch - 1,)),
        ],
        compiler_params=pltpu.CompilerParams(
            collective_id=0, has_side_effects=True, vmem_limit_bytes=16 * 1024 * 1024
        ),
        cost_estimate=pl.CostEstimate(flops=150_000_000, bytes_accessed=140_000, transcendentals=80_000),
    )(*arrays)


def solution(mesh):
    placed = (
        P("ch", "ctx"), P("ch", "ctx"), P("ch", "ctx"), P("ch", None), P("ch", None), P("ch"), P("ch"),
    )
    sizes = (mesh.shape["ctx"], mesh.shape["ch"])
    return jax.shard_map(
        functools.partial(body, sizes), mesh=mesh, in_specs=placed, out_specs=P("ch", "ctx"),
        check_vma=False,
    )
```

```python
import functools

import jax
import jax.numpy as jnp
from jax import lax
from jax.experimental import pallas as pl
from jax.experimental.pallas import tpu as pltpu
from jax.sharding import PartitionSpec as P

F32 = jnp.float32
BF16 = jnp.bfloat16
MESH = pl.DeviceIdType.MESH
CHUNK = 128


def split(value):
    high = value.astype(BF16)
    return high, (value - high.astype(F32)).astype(BF16)


def dot(left, right):
    return jnp.dot(left, right, preferred_element_type=F32)


def dot_nt(left, right):
    return lax.dot_general(left, right, (((1,), (1,)), ((), ())), preferred_element_type=F32)


def one_minus_exp(x):
    series = jnp.ones_like(x)
    for order in range(10, 1, -1):
        series = 1.0 - x * (1.0 / order) * series
    return jnp.where(x < 0.25, x * series, 1.0 - jnp.exp(-x))


def column(row, rows):
    width = row.shape[1]
    keep = lax.broadcasted_iota(jnp.int32, (rows, width), 0) == lax.broadcasted_iota(
        jnp.int32, (rows, width), 1
    )
    return jnp.sum(jnp.where(keep, row, 0.0), axis=1, keepdims=True)


def kernel(
    n_ctx, n_ch, query_hbm, key_hbm, value_hbm, residue_hbm, rate_hbm, skip_hbm, gain_hbm, out_ref,
    query_ref, key_ref, value_ref, residue_ref, rate_ref, skip_ref, gain_ref,
    toeplitz, spread, state, state_slots, square, square_slots,
    in_sems, state_send, state_recv, square_send, square_recv,
):
    my_ctx, my_ch = lax.axis_index("ctx"), lax.axis_index("ch")
    channels, block = query_ref.shape
    modes = rate_ref.shape[1]
    width = channels * modes
    chunks = block // CHUNK

    loads = [
        pltpu.make_async_copy(src, dst, in_sems.at[i])
        for i, (src, dst) in enumerate(
            (
                (rate_hbm, rate_ref), (residue_hbm, residue_ref), (key_hbm, key_ref),
                (value_hbm, value_ref), (skip_hbm, skip_ref), (gain_hbm, gain_ref),
                (query_hbm, query_ref),
            )
        )
    ]
    for load in loads:
        load.start()

    barrier = pltpu.get_barrier_semaphore()
    for step in range(1, n_ctx):
        pl.semaphore_signal(
            barrier, inc=1, device_id={"ctx": lax.rem(my_ctx + step, n_ctx)}, device_id_type=MESH
        )
    for step in range(1, n_ch):
        pl.semaphore_signal(
            barrier, inc=1, device_id={"ch": lax.rem(my_ch + step, n_ch)}, device_id_type=MESH
        )

    loads[0].wait()
    loads[1].wait()
    lane = lax.broadcasted_iota(jnp.int32, (channels, width), 1)
    own = lane // modes == lax.broadcasted_iota(jnp.int32, (channels, width), 0)
    mode_lane = lax.broadcasted_iota(jnp.int32, (modes, width), 1)
    mode_row = lax.broadcasted_iota(jnp.int32, (modes, width), 0)
    pick = (lax.rem(mode_lane, modes) == mode_row).astype(F32)
    tiled = jnp.dot(
        jnp.concatenate([rate_ref[...], residue_ref[...]], axis=0), pick,
        precision=lax.Precision.HIGHEST, preferred_element_type=F32,
    )
    rate_tiled, residue_tiled = tiled[:channels], tiled[channels:]
    rate_row = jnp.sum(jnp.where(own, rate_tiled, 0.0), axis=0, keepdims=True)
    place = lax.broadcasted_iota(jnp.int32, (CHUNK, width), 0).astype(F32)
    tail_high, tail_low = split(jnp.exp(-rate_row * (CHUNK - place)))
    chunk_decay = jnp.exp(-rate_row * float(CHUNK))

    loads[2].wait()
    loads[3].wait()
    pieces = [
        key_ref[:, k * CHUNK:(k + 1) * CHUNK] * value_ref[:, k * CHUNK:(k + 1) * CHUNK]
        for k in range(chunks)
    ]
    signal = jnp.concatenate(pieces, axis=0)
    update = dot(signal, tail_high) + dot(signal, tail_low)
    held = jnp.zeros((channels, width), F32)
    states = []
    for k in range(chunks):
        states.append(held)
        held = chunk_decay * held + update[k * channels:(k + 1) * channels]
    state[...] = jnp.sum(jnp.where(own, held, 0.0), axis=0, keepdims=True)

    pl.semaphore_wait(barrier, n_ctx + n_ch - 2)
    state_copies = [
        pltpu.make_async_remote_copy(
            src_ref=state, dst_ref=state_slots.at[step - 1],
            send_sem=state_send.at[step - 1], recv_sem=state_recv.at[step - 1],
            device_id={"ctx": lax.rem(my_ctx + step, n_ctx)}, device_id_type=MESH,
        )
        for step in range(1, n_ctx)
    ]
    for copy in state_copies:
        copy.start()

    head_high, head_low = split(jnp.exp(-rate_row * place))
    scaled = jnp.where(own, jnp.sqrt(one_minus_exp(2.0 * rate_tiled)) * residue_tiled, 0.0)
    scaled_high, scaled_low = split(scaled)
    taps = (
        dot_nt(scaled_high, head_high) + dot_nt(scaled_high, head_low)
        + dot_nt(scaled_low, head_high)
    )
    loads[4].wait()
    loads[5].wait()
    first = lax.broadcasted_iota(jnp.int32, (channels, CHUNK), 1) == 0
    taps = taps + jnp.where(first, column(skip_ref[...], channels), 0.0)
    gain = column(gain_ref[...], channels)
    causal = lax.broadcasted_iota(jnp.int32, (CHUNK, CHUNK), 1) >= lax.broadcasted_iota(
        jnp.int32, (CHUNK, CHUNK), 0
    )
    rows = lax.broadcasted_iota(jnp.int32, (channels, CHUNK), 0)
    for c in range(channels):
        rolled = pltpu.roll(
            jnp.broadcast_to(taps[c:c + 1], (CHUNK, CHUNK)), 0, 1, stride=1, stride_axis=0
        )
        toeplitz[c * CHUNK:(c + 1) * CHUNK, :] = jnp.where(causal, rolled, 0.0).astype(BF16)
        this = (rows == c).astype(F32).astype(BF16)
        for k in range(chunks):
            spread[k * channels:(k + 1) * channels, c * CHUNK:(c + 1) * CHUNK] = pieces[k] * this
    near = dot(spread[...], toeplitz[...])
    loads[6].wait()

    carry = jnp.zeros((1, width), F32)
    for step in range(1, n_ctx):
        state_copies[step - 1].wait_recv()
        weight = (my_ctx >= step).astype(F32)
        carry = carry + weight * jnp.exp(-rate_row * float(block * (step - 1))) * state_slots[step - 1]
    full = jnp.concatenate(
        [
            (states[k] + jnp.exp(-rate_row * float(CHUNK * k)) * carry) * scaled
            for k in range(chunks)
        ],
        axis=0,
    )
    full_high, full_low = split(full)
    conv = near + (
        dot_nt(full_high, head_high) + dot_nt(full_high, head_low) + dot_nt(full_low, head_high)
    )
    mixed = []
    for k in range(chunks):
        part = query_ref[:, k * CHUNK:(k + 1) * CHUNK].astype(F32) * conv[k * channels:(k + 1) * channels]
        mixed.append(part)
        square[k:k + 1, :] = jnp.sum(part * part, axis=0, keepdims=True)

    square_copies = [
        pltpu.make_async_remote_copy(
            src_ref=square, dst_ref=square_slots.at[step - 1],
            send_sem=square_send.at[step - 1], recv_sem=square_recv.at[step - 1],
            device_id={"ch": lax.rem(my_ch + step, n_ch)}, device_id_type=MESH,
        )
        for step in range(1, n_ch)
    ]
    for copy in square_copies:
        copy.start()
    total = square[...]
    for step in range(1, n_ch):
        square_copies[step - 1].wait_recv()
        total = total + square_slots[step - 1]
    scale = lax.rsqrt(total * (1.0 / (channels * n_ch)) + 1e-06)
    for k in range(chunks):
        out_ref[:, k * CHUNK:(k + 1) * CHUNK] = (mixed[k] * scale[k:k + 1] * gain).astype(BF16)
    for copy in state_copies + square_copies:
        copy.wait_send()


def body(mesh_shape, query, key_branch, value_branch, residue, rate, skip, gain):
    n_ctx, n_ch = mesh_shape
    channels, block = query.shape
    modes = rate.shape[1]
    width = channels * modes
    chunks = block // CHUNK
    arrays = tuple(pltpu.with_memory_space_constraint(a, pltpu.HBM) for a in (
        query, key_branch, value_branch, residue, rate,
        skip.reshape(1, channels), gain.reshape(1, channels),
    ))
    return pl.pallas_call(
        functools.partial(kernel, n_ctx, n_ch),
        out_shape=pltpu.VMEM((channels, block), BF16),
        in_specs=[pl.BlockSpec(memory_space=pltpu.HBM)] * len(arrays),
        out_specs=pl.BlockSpec(memory_space=pltpu.VMEM),
        scratch_shapes=[pltpu.VMEM(a.shape, a.dtype) for a in arrays] + [
            pltpu.VMEM((channels * CHUNK, CHUNK), BF16),
            pltpu.VMEM((chunks * channels, channels * CHUNK), BF16),
            pltpu.VMEM((1, width), F32),
            pltpu.VMEM((n_ctx - 1, 1, width), F32),
            pltpu.VMEM((chunks, CHUNK), F32),
            pltpu.VMEM((n_ch - 1, chunks, CHUNK), F32),
            pltpu.SemaphoreType.DMA((len(arrays),)),
            pltpu.SemaphoreType.DMA((n_ctx - 1,)),
            pltpu.SemaphoreType.DMA((n_ctx - 1,)),
            pltpu.SemaphoreType.DMA((n_ch - 1,)),
            pltpu.SemaphoreType.DMA((n_ch - 1,)),
        ],
        compiler_params=pltpu.CompilerParams(
            collective_id=0, has_side_effects=True
        ),
        cost_estimate=pl.CostEstimate(flops=150_000_000, bytes_accessed=140_000, transcendentals=80_000),
    )(*arrays)


def solution(mesh):
    placed = (
        P("ch", "ctx"), P("ch", "ctx"), P("ch", "ctx"), P("ch", None), P("ch", None), P("ch"), P("ch"),
    )
    sizes = (mesh.shape["ctx"], mesh.shape["ch"])
    return jax.shard_map(
        functools.partial(body, sizes), mesh=mesh, in_specs=placed, out_specs=P("ch", "ctx"),
        check_vma=False,
    )
```

```python
import functools

import jax
import jax.numpy as jnp
from jax import lax
from jax.experimental import pallas as pl
from jax.experimental.pallas import tpu as pltpu
from jax.sharding import PartitionSpec as P

F32 = jnp.float32
BF16 = jnp.bfloat16
MESH = pl.DeviceIdType.MESH
CHUNK = 128


def split(value):
    high = value.astype(BF16)
    return high, (value - high.astype(F32)).astype(BF16)


def dot(left, right):
    return jnp.dot(left, right, preferred_element_type=F32)


def dot_nt(left, right):
    return lax.dot_general(left, right, (((1,), (1,)), ((), ())), preferred_element_type=F32)


def one_minus_exp(x):
    series = jnp.ones_like(x)
    for order in range(10, 1, -1):
        series = 1.0 - x * (1.0 / order) * series
    return jnp.where(x < 0.25, x * series, 1.0 - jnp.exp(-x))


def column(row, rows):
    width = row.shape[1]
    keep = lax.broadcasted_iota(jnp.int32, (rows, width), 0) == lax.broadcasted_iota(
        jnp.int32, (rows, width), 1
    )
    return jnp.sum(jnp.where(keep, row, 0.0), axis=1, keepdims=True)


def kernel(
    n_ctx, n_ch, query_hbm, key_hbm, value_hbm, residue_hbm, rate_hbm, skip_hbm, gain_hbm, out_ref,
    query_ref, key_ref, value_ref, residue_ref, rate_ref, skip_ref, gain_ref,
    toeplitz, spread, state, state_slots, square, square_slots,
    in_sems, state_send, state_recv, square_send, square_recv,
):
    my_ctx, my_ch = lax.axis_index("ctx"), lax.axis_index("ch")
    channels, block = query_ref.shape
    modes = rate_ref.shape[1]
    width = channels * modes
    chunks = block // CHUNK

    loads = [
        pltpu.make_async_copy(src, dst, in_sems.at[i])
        for i, (src, dst) in enumerate(
            (
                (rate_hbm, rate_ref), (residue_hbm, residue_ref), (key_hbm, key_ref),
                (value_hbm, value_ref), (skip_hbm, skip_ref), (gain_hbm, gain_ref),
                (query_hbm, query_ref),
            )
        )
    ]
    loads[0].start()
    barrier = pltpu.get_barrier_semaphore()
    for step in range(1, n_ctx):
        @pl.when(my_ctx >= step)
        def greet():
            pl.semaphore_signal(
                barrier, inc=1, device_id={"ctx": my_ctx - step}, device_id_type=MESH
            )

        @pl.when(my_ctx < step)
        def clear():
            state_slots[step - 1] = jnp.zeros((1, width), F32)
    for step in range(1, n_ch):
        pl.semaphore_signal(
            barrier, inc=1, device_id={"ch": lax.rem(my_ch + step, n_ch)}, device_id_type=MESH
        )

    for load in loads[1:]:
        load.start()
    loads[0].wait()
    lane = lax.broadcasted_iota(jnp.int32, (channels, width), 1)
    own = lane // modes == lax.broadcasted_iota(jnp.int32, (channels, width), 0)
    rate_tiled = jnp.concatenate([rate_ref[...]] * channels, axis=1)
    rate_row = jnp.sum(jnp.where(own, rate_tiled, 0.0), axis=0, keepdims=True)
    place = lax.broadcasted_iota(jnp.int32, (CHUNK, width), 0).astype(F32)
    tail_high, tail_low = split(jnp.exp(-rate_row * (CHUNK - place)))
    chunk_decay = jnp.exp(-rate_row * float(CHUNK))

    loads[2].wait()
    loads[3].wait()
    pieces = [
        key_ref[:, k * CHUNK:(k + 1) * CHUNK] * value_ref[:, k * CHUNK:(k + 1) * CHUNK]
        for k in range(chunks)
    ]
    signal = jnp.concatenate(pieces, axis=0)
    update = dot(signal, tail_high) + dot(signal, tail_low)
    held = jnp.zeros((channels, width), F32)
    states = []
    for k in range(chunks):
        states.append(held)
        held = chunk_decay * held + update[k * channels:(k + 1) * channels]
    state[...] = jnp.sum(jnp.where(own, held, 0.0), axis=0, keepdims=True)

    pl.semaphore_wait(barrier, n_ctx - 1 - my_ctx + n_ch - 1)
    state_copies = [
        pltpu.make_async_remote_copy(
            src_ref=state, dst_ref=state_slots.at[step - 1],
            send_sem=state_send.at[step - 1], recv_sem=state_recv.at[step - 1],
            device_id={"ctx": lax.rem(my_ctx + step, n_ctx)}, device_id_type=MESH,
        )
        for step in range(1, n_ctx)
    ]
    for step in range(1, n_ctx):
        pl.when(my_ctx + step < n_ctx)(state_copies[step - 1].start)

    loads[1].wait()
    residue_tiled = jnp.concatenate([residue_ref[...]] * channels, axis=1)
    head_high, head_low = split(jnp.exp(-rate_row * place))
    scaled = jnp.where(own, jnp.sqrt(one_minus_exp(2.0 * rate_tiled)) * residue_tiled, 0.0)
    scaled_high, scaled_low = split(scaled)
    taps = (
        dot_nt(scaled_high, head_high) + dot_nt(scaled_high, head_low)
        + dot_nt(scaled_low, head_high)
    )
    loads[4].wait()
    loads[5].wait()
    first = lax.broadcasted_iota(jnp.int32, (channels, CHUNK), 1) == 0
    taps = taps + jnp.where(first, column(skip_ref[...], channels), 0.0)
    gain = column(gain_ref[...], channels)
    causal = lax.broadcasted_iota(jnp.int32, (CHUNK, CHUNK), 1) >= lax.broadcasted_iota(
        jnp.int32, (CHUNK, CHUNK), 0
    )
    rows = lax.broadcasted_iota(jnp.int32, (channels, CHUNK), 0)
    for c in range(channels):
        rolled = pltpu.roll(
            jnp.broadcast_to(taps[c:c + 1], (CHUNK, CHUNK)), 0, 1, stride=1, stride_axis=0
        )
        toeplitz[c * CHUNK:(c + 1) * CHUNK, :] = jnp.where(causal, rolled, 0.0).astype(BF16)
        this = (rows == c).astype(F32).astype(BF16)
        for k in range(chunks):
            spread[k * channels:(k + 1) * channels, c * CHUNK:(c + 1) * CHUNK] = pieces[k] * this
    near = dot(spread[...], toeplitz[...])
    loads[6].wait()

    carry = jnp.zeros((1, width), F32)
    for step in range(1, n_ctx):
        pl.when(my_ctx >= step)(state_copies[step - 1].wait_recv)
        carry = carry + jnp.exp(-rate_row * float(block * (step - 1))) * state_slots[step - 1]
    full = jnp.concatenate(
        [
            (states[k] + jnp.exp(-rate_row * float(CHUNK * k)) * carry) * scaled
            for k in range(chunks)
        ],
        axis=0,
    )
    full_high, full_low = split(full)
    conv = near + (
        dot_nt(full_high, head_high) + dot_nt(full_high, head_low) + dot_nt(full_low, head_high)
    )
    mixed = []
    for k in range(chunks):
        part = query_ref[:, k * CHUNK:(k + 1) * CHUNK].astype(F32) * conv[k * channels:(k + 1) * channels]
        mixed.append(part)
        square[k:k + 1, :] = jnp.sum(part * part, axis=0, keepdims=True)

    square_copies = [
        pltpu.make_async_remote_copy(
            src_ref=square, dst_ref=square_slots.at[step - 1],
            send_sem=square_send.at[step - 1], recv_sem=square_recv.at[step - 1],
            device_id={"ch": lax.rem(my_ch + step, n_ch)}, device_id_type=MESH,
        )
        for step in range(1, n_ch)
    ]
    for copy in square_copies:
        copy.start()
    total = square[...]
    for step in range(1, n_ch):
        square_copies[step - 1].wait_recv()
        total = total + square_slots[step - 1]
    scale = lax.rsqrt(total * (1.0 / (channels * n_ch)) + 1e-06)
    for k in range(chunks):
        out_ref[:, k * CHUNK:(k + 1) * CHUNK] = (mixed[k] * scale[k:k + 1] * gain).astype(BF16)
    for step in range(1, n_ctx):
        pl.when(my_ctx + step < n_ctx)(state_copies[step - 1].wait_send)
    for copy in square_copies:
        copy.wait_send()


def body(mesh_shape, query, key_branch, value_branch, residue, rate, skip, gain):
    n_ctx, n_ch = mesh_shape
    channels, block = query.shape
    modes = rate.shape[1]
    width = channels * modes
    chunks = block // CHUNK
    arrays = tuple(pltpu.with_memory_space_constraint(a, pltpu.HBM) for a in (
        query, key_branch, value_branch, residue, rate,
        skip.reshape(1, channels), gain.reshape(1, channels),
    ))
    return pl.pallas_call(
        functools.partial(kernel, n_ctx, n_ch),
        out_shape=pltpu.VMEM((channels, block), BF16),
        in_specs=[pl.BlockSpec(memory_space=pltpu.HBM)] * len(arrays),
        out_specs=pl.BlockSpec(memory_space=pltpu.VMEM),
        scratch_shapes=[pltpu.VMEM(a.shape, a.dtype) for a in arrays] + [
            pltpu.VMEM((channels * CHUNK, CHUNK), BF16),
            pltpu.VMEM((chunks * channels, channels * CHUNK), BF16),
            pltpu.VMEM((1, width), F32),
            pltpu.VMEM((n_ctx - 1, 1, width), F32),
            pltpu.VMEM((chunks, CHUNK), F32),
            pltpu.VMEM((n_ch - 1, chunks, CHUNK), F32),
            pltpu.SemaphoreType.DMA((len(arrays),)),
            pltpu.SemaphoreType.DMA((n_ctx - 1,)),
            pltpu.SemaphoreType.DMA((n_ctx - 1,)),
            pltpu.SemaphoreType.DMA((n_ch - 1,)),
            pltpu.SemaphoreType.DMA((n_ch - 1,)),
        ],
        compiler_params=pltpu.CompilerParams(
            collective_id=0, has_side_effects=True
        ),
        cost_estimate=pl.CostEstimate(flops=150_000_000, bytes_accessed=140_000, transcendentals=80_000),
    )(*arrays)


def solution(mesh):
    placed = (
        P("ch", "ctx"), P("ch", "ctx"), P("ch", "ctx"), P("ch", None), P("ch", None), P("ch"), P("ch"),
    )
    sizes = (mesh.shape["ctx"], mesh.shape["ch"])
    return jax.shard_map(
        functools.partial(body, sizes), mesh=mesh, in_specs=placed, out_specs=P("ch", "ctx"),
        check_vma=False,
    )
```

```python
import functools

import jax
import jax.numpy as jnp
from jax import lax
from jax.experimental import pallas as pl
from jax.experimental.pallas import tpu as pltpu
from jax.sharding import PartitionSpec as P

F32 = jnp.float32
BF16 = jnp.bfloat16
MESH = pl.DeviceIdType.MESH
CHUNK = 128


def split(value):
    high = value.astype(BF16)
    return high, (value - high.astype(F32)).astype(BF16)


def dot(left, right):
    return jnp.dot(left, right, preferred_element_type=F32)


def dot_nt(left, right):
    return lax.dot_general(left, right, (((1,), (1,)), ((), ())), preferred_element_type=F32)


def one_minus_exp(x):
    series = jnp.ones_like(x)
    for order in range(10, 1, -1):
        series = 1.0 - x * (1.0 / order) * series
    return jnp.where(x < 0.25, x * series, 1.0 - jnp.exp(-x))


def column(row, rows):
    width = row.shape[1]
    keep = lax.broadcasted_iota(jnp.int32, (rows, width), 0) == lax.broadcasted_iota(
        jnp.int32, (rows, width), 1
    )
    return jnp.sum(jnp.where(keep, row, 0.0), axis=1, keepdims=True)


def kernel(
    n_ctx, n_ch, query_hbm, key_hbm, value_hbm, residue_hbm, rate_hbm, skip_hbm, gain_hbm, out_ref,
    query_ref, key_ref, value_ref, residue_ref, rate_ref, skip_ref, gain_ref,
    toeplitz, spread, state, state_slots, square, square_slots,
    in_sems, state_send, state_recv, square_send, square_recv,
):
    my_ctx, my_ch = lax.axis_index("ctx"), lax.axis_index("ch")
    channels, block = query_ref.shape
    modes = rate_ref.shape[1]
    width = channels * modes
    chunks = block // CHUNK

    loads = [
        pltpu.make_async_copy(src, dst, in_sems.at[i])
        for i, (src, dst) in enumerate(
            (
                (rate_hbm, rate_ref), (residue_hbm, residue_ref), (key_hbm, key_ref),
                (value_hbm, value_ref), (skip_hbm, skip_ref), (gain_hbm, gain_ref),
                (query_hbm, query_ref),
            )
        )
    ]
    for i in (0, 2, 3):
        loads[i].start()
    barrier = pltpu.get_barrier_semaphore()
    for step in range(1, n_ctx):
        @pl.when(my_ctx >= step)
        def greet():
            pl.semaphore_signal(
                barrier, inc=1, device_id={"ctx": my_ctx - step}, device_id_type=MESH
            )

        @pl.when(my_ctx < step)
        def clear():
            state_slots[step - 1] = jnp.zeros((1, width), F32)
    for step in range(1, n_ch):
        pl.semaphore_signal(
            barrier, inc=1, device_id={"ch": lax.rem(my_ch + step, n_ch)}, device_id_type=MESH
        )

    for i in (1, 4, 5, 6):
        loads[i].start()
    loads[0].wait()
    lane = lax.broadcasted_iota(jnp.int32, (channels, width), 1)
    own = lane // modes == lax.broadcasted_iota(jnp.int32, (channels, width), 0)
    rate_tiled = jnp.concatenate([rate_ref[...]] * channels, axis=1)
    rate_row = jnp.sum(jnp.where(own, rate_tiled, 0.0), axis=0, keepdims=True)
    fine = lax.broadcasted_iota(jnp.int32, (8, width), 0).astype(F32)
    coarse = 8.0 * lax.broadcasted_iota(jnp.int32, (CHUNK // 8, width), 0).astype(F32)
    tail_fine = jnp.exp(-rate_row * (8.0 - fine))
    powers = jnp.exp(-rate_row * coarse)
    tail_high, tail_low = split(
        jnp.concatenate([tail_fine * powers[i:i + 1] for i in reversed(range(CHUNK // 8))], axis=0)
    )
    chunk_decay = jnp.exp(-rate_row * float(CHUNK))

    loads[2].wait()
    loads[3].wait()
    pieces = [
        key_ref[:, k * CHUNK:(k + 1) * CHUNK] * value_ref[:, k * CHUNK:(k + 1) * CHUNK]
        for k in range(chunks)
    ]
    signal = jnp.concatenate(pieces, axis=0)
    update = dot(signal, tail_high) + dot(signal, tail_low)
    held = jnp.zeros((channels, width), F32)
    states = []
    for k in range(chunks):
        states.append(held)
        held = chunk_decay * held + update[k * channels:(k + 1) * channels]
    state[...] = jnp.sum(jnp.where(own, held, 0.0), axis=0, keepdims=True)

    loads[1].wait()
    residue_tiled = jnp.concatenate([residue_ref[...]] * channels, axis=1)
    head_fine = jnp.exp(-rate_row * fine)
    head_high, head_low = split(
        jnp.concatenate([head_fine * powers[i:i + 1] for i in range(CHUNK // 8)], axis=0)
    )
    scaled = jnp.where(own, jnp.sqrt(one_minus_exp(2.0 * rate_tiled)) * residue_tiled, 0.0)
    scaled_high, scaled_low = split(scaled)
    taps = (
        dot_nt(scaled_high, head_high) + dot_nt(scaled_high, head_low)
        + dot_nt(scaled_low, head_high)
    )
    pl.semaphore_wait(barrier, n_ctx - 1 - my_ctx + n_ch - 1)
    state_copies = [
        pltpu.make_async_remote_copy(
            src_ref=state, dst_ref=state_slots.at[step - 1],
            send_sem=state_send.at[step - 1], recv_sem=state_recv.at[step - 1],
            device_id={"ctx": lax.rem(my_ctx + step, n_ctx)}, device_id_type=MESH,
        )
        for step in range(1, n_ctx)
    ]
    for step in range(1, n_ctx):
        pl.when(my_ctx + step < n_ctx)(state_copies[step - 1].start)

    loads[4].wait()
    loads[5].wait()
    first = lax.broadcasted_iota(jnp.int32, (channels, CHUNK), 1) == 0
    taps = taps + jnp.where(first, column(skip_ref[...], channels), 0.0)
    gain = column(gain_ref[...], channels)
    causal = lax.broadcasted_iota(jnp.int32, (CHUNK, CHUNK), 1) >= lax.broadcasted_iota(
        jnp.int32, (CHUNK, CHUNK), 0
    )
    rows = lax.broadcasted_iota(jnp.int32, (channels, CHUNK), 0)
    for c in range(channels):
        rolled = pltpu.roll(
            jnp.broadcast_to(taps[c:c + 1], (CHUNK, CHUNK)), 0, 1, stride=1, stride_axis=0
        )
        toeplitz[c * CHUNK:(c + 1) * CHUNK, :] = jnp.where(causal, rolled, 0.0).astype(BF16)
        this = (rows == c).astype(F32).astype(BF16)
        for k in range(chunks):
            spread[k * channels:(k + 1) * channels, c * CHUNK:(c + 1) * CHUNK] = pieces[k] * this
    reach = [jnp.exp(-rate_row * float(CHUNK * k)) * scaled for k in range(chunks)]
    ready = [states[k] * scaled for k in range(chunks)]
    weights = [jnp.exp(-rate_row * float(block * step)) for step in range(n_ctx - 1)]
    near = dot(spread[...], toeplitz[...])
    loads[6].wait()

    carry = jnp.zeros((1, width), F32)
    for step in range(1, n_ctx):
        pl.when(my_ctx >= step)(state_copies[step - 1].wait_recv)
        carry = carry + weights[step - 1] * state_slots[step - 1]
    full = jnp.concatenate([ready[k] + reach[k] * carry for k in range(chunks)], axis=0)
    full_high, full_low = split(full)
    conv = near + (
        dot_nt(full_high, head_high) + dot_nt(full_high, head_low) + dot_nt(full_low, head_high)
    )
    mixed = []
    for k in range(chunks):
        part = query_ref[:, k * CHUNK:(k + 1) * CHUNK].astype(F32) * conv[k * channels:(k + 1) * channels]
        mixed.append(part)
        square[k:k + 1, :] = jnp.sum(part * part, axis=0, keepdims=True)

    square_copies = [
        pltpu.make_async_remote_copy(
            src_ref=square, dst_ref=square_slots.at[step - 1],
            send_sem=square_send.at[step - 1], recv_sem=square_recv.at[step - 1],
            device_id={"ch": lax.rem(my_ch + step, n_ch)}, device_id_type=MESH,
        )
        for step in range(1, n_ch)
    ]
    for copy in square_copies:
        copy.start()
    total = square[...]
    for step in range(1, n_ch):
        square_copies[step - 1].wait_recv()
        total = total + square_slots[step - 1]
    scale = lax.rsqrt(total * (1.0 / (channels * n_ch)) + 1e-06)
    for k in range(chunks):
        out_ref[:, k * CHUNK:(k + 1) * CHUNK] = (mixed[k] * scale[k:k + 1] * gain).astype(BF16)
    for step in range(1, n_ctx):
        pl.when(my_ctx + step < n_ctx)(state_copies[step - 1].wait_send)
    for copy in square_copies:
        copy.wait_send()


def body(mesh_shape, query, key_branch, value_branch, residue, rate, skip, gain):
    n_ctx, n_ch = mesh_shape
    channels, block = query.shape
    modes = rate.shape[1]
    width = channels * modes
    chunks = block // CHUNK
    arrays = tuple(pltpu.with_memory_space_constraint(a, pltpu.HBM) for a in (
        query, key_branch, value_branch, residue, rate,
        skip.reshape(1, channels), gain.reshape(1, channels),
    ))
    return pl.pallas_call(
        functools.partial(kernel, n_ctx, n_ch),
        out_shape=pltpu.VMEM((channels, block), BF16),
        in_specs=[pl.BlockSpec(memory_space=pltpu.HBM)] * len(arrays),
        out_specs=pl.BlockSpec(memory_space=pltpu.VMEM),
        scratch_shapes=[pltpu.VMEM(a.shape, a.dtype) for a in arrays] + [
            pltpu.VMEM((channels * CHUNK, CHUNK), BF16),
            pltpu.VMEM((chunks * channels, channels * CHUNK), BF16),
            pltpu.VMEM((1, width), F32),
            pltpu.VMEM((n_ctx - 1, 1, width), F32),
            pltpu.VMEM((chunks, CHUNK), F32),
            pltpu.VMEM((n_ch - 1, chunks, CHUNK), F32),
            pltpu.SemaphoreType.DMA((len(arrays),)),
            pltpu.SemaphoreType.DMA((n_ctx - 1,)),
            pltpu.SemaphoreType.DMA((n_ctx - 1,)),
            pltpu.SemaphoreType.DMA((n_ch - 1,)),
            pltpu.SemaphoreType.DMA((n_ch - 1,)),
        ],
        compiler_params=pltpu.CompilerParams(
            collective_id=0, has_side_effects=True
        ),
        cost_estimate=pl.CostEstimate(flops=150_000_000, bytes_accessed=140_000, transcendentals=80_000),
    )(*arrays)


def solution(mesh):
    placed = (
        P("ch", "ctx"), P("ch", "ctx"), P("ch", "ctx"), P("ch", None), P("ch", None), P("ch"), P("ch"),
    )
    sizes = (mesh.shape["ctx"], mesh.shape["ch"])
    return jax.shard_map(
        functools.partial(body, sizes), mesh=mesh, in_specs=placed, out_specs=P("ch", "ctx"),
        check_vma=False,
    )
```

```python
import functools

import jax
import jax.numpy as jnp
from jax import lax
from jax.experimental import pallas as pl
from jax.experimental.pallas import tpu as pltpu
from jax.sharding import PartitionSpec as P

F32 = jnp.float32
BF16 = jnp.bfloat16
MESH = pl.DeviceIdType.MESH
CHUNK = 128


def split(value):
    high = value.astype(BF16)
    return high, (value - high.astype(F32)).astype(BF16)


def dot(left, right):
    return jnp.dot(left, right, preferred_element_type=F32)


def dot_nt(left, right):
    return lax.dot_general(left, right, (((1,), (1,)), ((), ())), preferred_element_type=F32)


def one_minus_exp(x):
    series = jnp.ones_like(x)
    for order in range(10, 1, -1):
        series = 1.0 - x * (1.0 / order) * series
    return jnp.where(x < 0.25, x * series, 1.0 - jnp.exp(-x))


def column(row, rows):
    width = row.shape[1]
    keep = lax.broadcasted_iota(jnp.int32, (rows, width), 0) == lax.broadcasted_iota(
        jnp.int32, (rows, width), 1
    )
    return jnp.sum(jnp.where(keep, row, 0.0), axis=1, keepdims=True)


def kernel(
    n_ctx, n_ch, query_hbm, key_hbm, value_hbm, residue_hbm, rate_hbm, skip_hbm, gain_hbm, out_ref,
    query_ref, key_ref, value_ref, residue_ref, rate_ref, skip_ref, gain_ref,
    toeplitz, spread, state, state_slots, square, square_slots,
    in_sems, state_send, state_recv, square_send, square_recv,
):
    my_ctx, my_ch = lax.axis_index("ctx"), lax.axis_index("ch")
    channels, block = query_ref.shape
    modes = rate_ref.shape[1]
    width = channels * modes
    chunks = block // CHUNK

    loads = [
        pltpu.make_async_copy(src, dst, in_sems.at[i])
        for i, (src, dst) in enumerate(
            (
                (rate_hbm, rate_ref), (residue_hbm, residue_ref), (key_hbm, key_ref),
                (value_hbm, value_ref), (skip_hbm, skip_ref), (gain_hbm, gain_ref),
                (query_hbm, query_ref),
            )
        )
    ]
    for i in (0, 2, 3):
        loads[i].start()
    barrier = pltpu.get_barrier_semaphore()
    for step in range(1, n_ctx):
        @pl.when(my_ctx >= step)
        def greet():
            pl.semaphore_signal(
                barrier, inc=1, device_id={"ctx": my_ctx - step}, device_id_type=MESH
            )

        @pl.when(my_ctx < step)
        def clear():
            state_slots[step - 1] = jnp.zeros((1, width), F32)
    for step in range(1, n_ch):
        pl.semaphore_signal(
            barrier, inc=1, device_id={"ch": lax.rem(my_ch + step, n_ch)}, device_id_type=MESH
        )

    for i in (1, 4, 5, 6):
        loads[i].start()
    loads[0].wait()
    lane = lax.broadcasted_iota(jnp.int32, (channels, width), 1)
    own = lane // modes == lax.broadcasted_iota(jnp.int32, (channels, width), 0)
    rate_tiled = jnp.concatenate([rate_ref[...]] * channels, axis=1)
    rate_row = jnp.sum(jnp.where(own, rate_tiled, 0.0), axis=0, keepdims=True)
    fine = lax.broadcasted_iota(jnp.int32, (8, width), 0).astype(F32)
    coarse = 8.0 * lax.broadcasted_iota(jnp.int32, (CHUNK // 8, width), 0).astype(F32)
    tail_fine = jnp.exp(-rate_row * (8.0 - fine))
    powers = jnp.exp(-rate_row * coarse)
    tail_high, tail_low = split(
        jnp.concatenate([tail_fine * powers[i:i + 1] for i in reversed(range(CHUNK // 8))], axis=0)
    )
    chunk_decay = jnp.exp(-rate_row * float(CHUNK))

    loads[2].wait()
    loads[3].wait()
    pieces = [
        key_ref[:, k * CHUNK:(k + 1) * CHUNK] * value_ref[:, k * CHUNK:(k + 1) * CHUNK]
        for k in range(chunks)
    ]
    signal = jnp.concatenate(pieces, axis=0)
    update = dot(signal, tail_high) + dot(signal, tail_low)
    held = jnp.zeros((channels, width), F32)
    states = []
    for k in range(chunks):
        states.append(held)
        held = chunk_decay * held + update[k * channels:(k + 1) * channels]
    state[...] = jnp.sum(jnp.where(own, held, 0.0), axis=0, keepdims=True)

    loads[1].wait()
    residue_tiled = jnp.concatenate([residue_ref[...]] * channels, axis=1)
    head_fine = jnp.exp(-rate_row * fine)
    head_high, head_low = split(
        jnp.concatenate([head_fine * powers[i:i + 1] for i in range(CHUNK // 8)], axis=0)
    )
    scaled = jnp.where(own, jnp.sqrt(one_minus_exp(2.0 * rate_tiled)) * residue_tiled, 0.0)
    scaled_high, scaled_low = split(scaled)
    taps = (
        dot_nt(scaled_high, head_high) + dot_nt(scaled_high, head_low)
        + dot_nt(scaled_low, head_high)
    )
    pl.semaphore_wait(barrier, n_ctx - 1 - my_ctx + n_ch - 1)
    state_copies = [
        pltpu.make_async_remote_copy(
            src_ref=state, dst_ref=state_slots.at[step - 1],
            send_sem=state_send.at[step - 1], recv_sem=state_recv.at[step - 1],
            device_id={"ctx": lax.rem(my_ctx + step, n_ctx)}, device_id_type=MESH,
        )
        for step in range(1, n_ctx)
    ]
    for step in reversed(range(1, n_ctx)):
        pl.when(my_ctx + step < n_ctx)(state_copies[step - 1].start)

    loads[4].wait()
    loads[5].wait()
    first = lax.broadcasted_iota(jnp.int32, (channels, CHUNK), 1) == 0
    taps = taps + jnp.where(first, column(skip_ref[...], channels), 0.0)
    gain = column(gain_ref[...], channels)
    causal = lax.broadcasted_iota(jnp.int32, (CHUNK, CHUNK), 1) >= lax.broadcasted_iota(
        jnp.int32, (CHUNK, CHUNK), 0
    )
    rows = lax.broadcasted_iota(jnp.int32, (channels, CHUNK), 0)
    for c in range(channels):
        rolled = pltpu.roll(
            jnp.broadcast_to(taps[c:c + 1], (CHUNK, CHUNK)), 0, 1, stride=1, stride_axis=0
        )
        toeplitz[c * CHUNK:(c + 1) * CHUNK, :] = jnp.where(causal, rolled, 0.0).astype(BF16)
        this = (rows == c).astype(F32).astype(BF16)
        for k in range(chunks):
            spread[k * channels:(k + 1) * channels, c * CHUNK:(c + 1) * CHUNK] = pieces[k] * this
    reach = [jnp.exp(-rate_row * float(CHUNK * k)) * scaled for k in range(chunks)]
    ready = [states[k] * scaled for k in range(chunks)]
    weights = [jnp.exp(-rate_row * float(block * step)) for step in range(n_ctx - 1)]
    near = dot(spread[...], toeplitz[...])
    loads[6].wait()

    carry = jnp.zeros((1, width), F32)
    for step in range(1, n_ctx):
        pl.when(my_ctx >= step)(state_copies[step - 1].wait_recv)
        carry = carry + weights[step - 1] * state_slots[step - 1]
    full = jnp.concatenate([ready[k] + reach[k] * carry for k in range(chunks)], axis=0)
    full_high, full_low = split(full)
    conv = near + (
        dot_nt(full_high, head_high) + dot_nt(full_high, head_low) + dot_nt(full_low, head_high)
    )
    mixed = []
    for k in range(chunks):
        part = query_ref[:, k * CHUNK:(k + 1) * CHUNK].astype(F32) * conv[k * channels:(k + 1) * channels]
        mixed.append(part)
        square[k:k + 1, :] = jnp.sum(part * part, axis=0, keepdims=True)

    square_copies = [
        pltpu.make_async_remote_copy(
            src_ref=square, dst_ref=square_slots.at[step - 1],
            send_sem=square_send.at[step - 1], recv_sem=square_recv.at[step - 1],
            device_id={"ch": lax.rem(my_ch + step, n_ch)}, device_id_type=MESH,
        )
        for step in range(1, n_ch)
    ]
    for copy in reversed(square_copies):
        copy.start()
    total = square[...]
    for step in range(1, n_ch):
        square_copies[step - 1].wait_recv()
        total = total + square_slots[step - 1]
    scale = lax.rsqrt(total * (1.0 / (channels * n_ch)) + 1e-06)
    for k in range(chunks):
        out_ref[:, k * CHUNK:(k + 1) * CHUNK] = (mixed[k] * scale[k:k + 1] * gain).astype(BF16)
    for step in range(1, n_ctx):
        pl.when(my_ctx + step < n_ctx)(state_copies[step - 1].wait_send)
    for copy in square_copies:
        copy.wait_send()


def body(mesh_shape, query, key_branch, value_branch, residue, rate, skip, gain):
    n_ctx, n_ch = mesh_shape
    channels, block = query.shape
    modes = rate.shape[1]
    width = channels * modes
    chunks = block // CHUNK
    arrays = tuple(pltpu.with_memory_space_constraint(a, pltpu.HBM) for a in (
        query, key_branch, value_branch, residue, rate,
        skip.reshape(1, channels), gain.reshape(1, channels),
    ))
    return pl.pallas_call(
        functools.partial(kernel, n_ctx, n_ch),
        out_shape=pltpu.VMEM((channels, block), BF16),
        in_specs=[pl.BlockSpec(memory_space=pltpu.HBM)] * len(arrays),
        out_specs=pl.BlockSpec(memory_space=pltpu.VMEM),
        scratch_shapes=[pltpu.VMEM(a.shape, a.dtype) for a in arrays] + [
            pltpu.VMEM((channels * CHUNK, CHUNK), BF16),
            pltpu.VMEM((chunks * channels, channels * CHUNK), BF16),
            pltpu.VMEM((1, width), F32),
            pltpu.VMEM((n_ctx - 1, 1, width), F32),
            pltpu.VMEM((chunks, CHUNK), F32),
            pltpu.VMEM((n_ch - 1, chunks, CHUNK), F32),
            pltpu.SemaphoreType.DMA((len(arrays),)),
            pltpu.SemaphoreType.DMA((n_ctx - 1,)),
            pltpu.SemaphoreType.DMA((n_ctx - 1,)),
            pltpu.SemaphoreType.DMA((n_ch - 1,)),
            pltpu.SemaphoreType.DMA((n_ch - 1,)),
        ],
        compiler_params=pltpu.CompilerParams(
            collective_id=0, has_side_effects=True
        ),
        cost_estimate=pl.CostEstimate(flops=150_000_000, bytes_accessed=140_000, transcendentals=80_000),
    )(*arrays)


def solution(mesh):
    placed = (
        P("ch", "ctx"), P("ch", "ctx"), P("ch", "ctx"), P("ch", None), P("ch", None), P("ch"), P("ch"),
    )
    sizes = (mesh.shape["ctx"], mesh.shape["ch"])
    return jax.shard_map(
        functools.partial(body, sizes), mesh=mesh, in_specs=placed, out_specs=P("ch", "ctx"),
        check_vma=False,
    )
```
